256 devices in a mesh: adapter: 64 (over z, y, core), tensor: 4 (over x).
Axes of the slice: x: 4, y: 4, z: 8, core: 2. Of those that a mesh axis runs over, the one named last changes fastest.
Arguments:
- inputs: bfloat16 [32768, 5120], P('adapter', 'tensor'), may hold values from -6 to 6
- grad_key: bfloat16 [32768, 1024], P('adapter', 'tensor'), may hold values from -6 to 6
- grad_value: bfloat16 [32768, 1024], P('adapter', 'tensor'), may hold values from -6 to 6
- weight_key: bfloat16 [5120, 1024], P(None, 'tensor'), may hold values from -0.1875 to 0.1875
- weight_value: bfloat16 [5120, 1024], P(None, 'tensor'), may hold values from -0.1875 to 0.1875
- down_key: bfloat16 [1024, 16, 5120], P('adapter', None, 'tensor'), may hold values from -0.078125 to 0.078125
- down_value: bfloat16 [1024, 16, 5120], P('adapter', None, 'tensor'), may hold values from -0.078125 to 0.078125
- up_key: bfloat16 [1024, 16, 1024], P('adapter', None, 'tensor'), may hold values from -0.1875 to 0.1875
- up_value: bfloat16 [1024, 16, 1024], P('adapter', None, 'tensor'), may hold values from -0.1875 to 0.1875
- adapter_ids: int32 [32768], P('adapter'), may hold values from 0 to 1023, as said below
Outputs:
- input_gradient: bfloat16 [32768, 5120], P('adapter', 'tensor')
- grad_down_key: float32 [1024, 16, 5120], P('adapter', None, 'tensor')
- grad_down_value: float32 [1024, 16, 5120], P('adapter', None, 'tensor')
- up_key_gradient: float32 [1024, 16, 1024], P('adapter', None, 'tensor')
- up_value_gradient: float32 [1024, 16, 1024], P('adapter', None, 'tensor')
The draws below stay inside these ranges and needn't reach their ends.
Inputs may be any that keep to these rules, and one draw needn't show every extreme that they name: In each aligned block of 512 tokens (those of one index of adapter), at most 16 tokens have adapters of one owner (adapter_ids // 16), and in every block exactly 16 tokens have adapters of one owner that is the same for all blocks.
All inputs are finite; a program needn't handle non-finite values.
Results may differ from the reference program's by a relative error of at most 0.0034.
Values may be sent and summed in bfloat16 or wider, within the bound.
No kernel may reach another device: no remote copies, remote signals or barrier semaphores. Data moves between devices by JAX's collectives and lax.ppermute only.
A program may use at most 128 MiB of HBM per device.

```python
import jax
import jax.numpy as jnp
from jax import lax

D = 5120
KV = 1024
R = 16
TOK_DEV = 512
ADP_DEV = 16
ADAPTERS = 1024
TOKENS = 32768
N_ADAPTER = 64


def draw_adapter_ids(key, part):
    key = jax.random.fold_in(key, 7)
    capacity = max(2, 2 * TOK_DEV // N_ADAPTER)
    pairs = N_ADAPTER * capacity
    key_hot, key_heat, key_noise, key_order, key_within = jax.random.split(key, 5)
    hottest = jax.random.randint(key_hot, (), 0, N_ADAPTER)
    heat = jax.random.randint(key_heat, (N_ADAPTER,), 0, 2 ** 15)
    pair_owner = jnp.arange(pairs, dtype=jnp.int32) // capacity
    offset = jnp.where(pair_owner == hottest, 2 ** 17, heat[pair_owner])
    noise = jax.random.randint(key_noise, (N_ADAPTER, pairs), 0, 2 ** 16)
    scores = (offset[None, :] + noise) * pairs + jnp.arange(pairs, dtype=jnp.int32)[None, :]
    _, picked = lax.top_k(scores, TOK_DEV)
    owners = pair_owner[picked]
    shuffle = jax.random.randint(key_order, (N_ADAPTER, TOK_DEV), 0, 2 ** 16) * TOK_DEV + jnp.arange(TOK_DEV, dtype=jnp.int32)[None, :]
    _, order = lax.top_k(shuffle, TOK_DEV)
    owners = jnp.take_along_axis(owners, order, axis=1)
    within = jax.random.randint(key_within, (N_ADAPTER, TOK_DEV), 0, ADP_DEV)
    return (owners * ADP_DEV + within).reshape(-1).astype(jnp.int32)


def block_levels(stream_key, dims, shards, least, high):
    level = 1.0
    for axis_at, shards_of in shards:
        draws = jax.random.uniform(jax.random.fold_in(jax.random.fold_in(stream_key, 6), axis_at), (shards_of,), jnp.float32, least / len(shards), high / len(shards))
        level = level * jnp.repeat(jnp.exp(draws), dims[axis_at] // shards_of).reshape((-1,) + (1,) * (len(dims) - 1 - axis_at))
    return level


def normal_values(key, dims, spread, limit, shards=(), kind=jnp.bfloat16):
    array = jax.random.normal(key, dims, jnp.float32) * spread
    if len(shards) > 0:
        array = block_levels(key, dims, shards, -0.22, 0.18) * array
    return jnp.clip(array, min=-limit, max=limit).astype(kind)


def setup_inputs(seed: int = 0) -> dict:
    splits = jax.random.split(jax.random.key(seed), 11)
    return {
        "inputs": normal_values(splits[0], (TOKENS, D), 1.0, 6.0, ((0, 64), (1, 4))),
        "grad_key": normal_values(splits[1], (TOKENS, KV), 1.0, 6.0, ((0, 64), (1, 4))),
        "grad_value": normal_values(splits[2], (TOKENS, KV), 1.0, 6.0, ((0, 64), (1, 4))),
        "weight_key": normal_values(splits[3], (D, KV), KV ** -0.5, 0.1875, ((1, 4),)),
        "weight_value": normal_values(splits[4], (D, KV), KV ** -0.5, 0.1875, ((1, 4),)),
        "down_key": normal_values(splits[5], (ADAPTERS, R, D), D ** -0.5, 0.078125, ((0, 64), (2, 4))),
        "down_value": normal_values(splits[6], (ADAPTERS, R, D), D ** -0.5, 0.078125, ((0, 64), (2, 4))),
        "up_key": normal_values(splits[7], (ADAPTERS, R, KV), KV ** -0.5, 0.1875, ((0, 64), (2, 4))),
        "up_value": normal_values(splits[8], (ADAPTERS, R, KV), KV ** -0.5, 0.1875, ((0, 64), (2, 4))),
        "adapter_ids": draw_adapter_ids(jax.random.fold_in(splits[10], 71), 0),
    }


adapter_scale = 2.0


def reference(inputs, grad_key, grad_value, weight_key, weight_value, down_key, down_value, up_key, up_value, adapter_ids):
    blocks = TOKENS // TOK_DEV
    input_blocks = inputs.reshape(blocks, TOK_DEV, D)
    key_blocks = grad_key.reshape(blocks, TOK_DEV, KV)
    value_blocks = grad_value.reshape(blocks, TOK_DEV, KV)
    id_blocks = adapter_ids.reshape(blocks, TOK_DEV)

    def accumulate(totals, pieces):
        acc_down_key, acc_down_value, accumulated_up_key, accumulated_up_value = totals
        block_inputs, block_key, block_value, block_adapter_index = pieces
        input_float = block_inputs.astype(jnp.float32)
        key_single_float = block_key.astype(jnp.float32)
        value_single_float = block_value.astype(jnp.float32)
        selected_down_key = down_key[block_adapter_index].astype(jnp.float32)
        chosen_down_value = down_value[block_adapter_index].astype(jnp.float32)
        selected_up_key = up_key[block_adapter_index].astype(jnp.float32)
        selected_up_value = up_value[block_adapter_index].astype(jnp.float32)
        reduced_key = jnp.einsum('td,trd->tr', input_float, selected_down_key).astype(jnp.bfloat16)
        reduced_value = jnp.einsum('td,trd->tr', input_float, chosen_down_value).astype(jnp.bfloat16)
        backward_key = (adapter_scale * jnp.einsum('ei,eai->ea', key_single_float, selected_up_key)).astype(jnp.bfloat16)
        backward_value = (adapter_scale * jnp.einsum('ei,eai->ea', value_single_float, selected_up_value)).astype(jnp.bfloat16)
        backward_key_float = backward_key.astype(jnp.float32)
        back_value_float = backward_value.astype(jnp.float32)
        acc_down_key = acc_down_key.at[block_adapter_index].add(jnp.einsum('tr,td->trd', backward_key_float, input_float))
        acc_down_value = acc_down_value.at[block_adapter_index].add(jnp.einsum('tr,td->trd', back_value_float, input_float))
        accumulated_up_key = accumulated_up_key.at[block_adapter_index].add(adapter_scale * jnp.einsum('wp,wv->wpv', reduced_key.astype(jnp.float32), key_single_float))
        accumulated_up_value = accumulated_up_value.at[block_adapter_index].add(adapter_scale * jnp.einsum('wp,wv->wpv', reduced_value.astype(jnp.float32), value_single_float))
        adapter_input_gradient = (jnp.einsum('me,mey->my', backward_key_float, selected_down_key)
                     + jnp.einsum('me,mey->my', back_value_float, chosen_down_value)).astype(jnp.bfloat16)
        frozen_input_gradient = jnp.dot(block_key, weight_key.T, preferred_element_type=jnp.float32)
        frozen_input_gradient = frozen_input_gradient + jnp.dot(block_value, weight_value.T, preferred_element_type=jnp.float32)
        block_input_gradient = (frozen_input_gradient + adapter_input_gradient.astype(jnp.float32)).astype(jnp.bfloat16)
        return (acc_down_key, acc_down_value, accumulated_up_key, accumulated_up_value), block_input_gradient

    start = (jnp.zeros((ADAPTERS, R, D), jnp.float32), jnp.zeros((ADAPTERS, R, D), jnp.float32),
             jnp.zeros((ADAPTERS, R, KV), jnp.float32), jnp.zeros((ADAPTERS, R, KV), jnp.float32))
    totals, grads = lax.scan(accumulate, start, (input_blocks, key_blocks, value_blocks, id_blocks))
    input_gradient = grads.reshape(TOKENS, D)
    return (input_gradient, totals[0], totals[1], totals[2], totals[3])
```

```python
import functools

import jax
import jax.numpy as jnp
from jax import lax
from jax.experimental import pallas as pl
from jax.experimental.pallas import tpu as pltpu
from jax.sharding import PartitionSpec as P

adapter_scale = 2.0

SLOTS = 16
MIB = 1 << 20
bf16 = jnp.bfloat16
f32 = jnp.float32


def call(kernel, outs, name, vmem=48, smem=0, scratch=(), after=(), anywhere=False, alias={}):
    def run(*args):
        specs = [
            pl.BlockSpec(memory_space=pltpu.SMEM if i < smem else pl.ANY if anywhere else pltpu.VMEM)
            for i in range(len(args))
        ]
        specs += [pl.BlockSpec(memory_space=pl.ANY)] * len(after)

        def body(*refs):
            kernel(*refs[: len(args)], *refs[len(args) + len(after) :])

        return pl.pallas_call(
            body,
            out_shape=[jax.ShapeDtypeStruct(s, d) for s, d in outs],
            in_specs=specs,
            out_specs=[pl.BlockSpec(memory_space=pl.ANY if anywhere else pltpu.VMEM) for _ in outs],
            scratch_shapes=list(scratch),
            compiler_params=pltpu.CompilerParams(vmem_limit_bytes=vmem * MIB),
            input_output_aliases=alias,
            name=name,
        )(*args, *after)

    return run


def dot(a, b, ca, cb):
    return lax.dot_general(a, b, (((ca,), (cb,)), ((), ())), preferred_element_type=f32)


def route_kernel(ids_ref, key_ref, value_ref, route_ref, sent_ref):
    ids = ids_ref[...]
    tokens = ids.shape[1]
    slots = route_ref.shape[0]
    owner = ids >> 4
    within = ids & 15
    owner_hot = lax.broadcasted_iota(jnp.int32, (slots // SLOTS, tokens), 0) == owner
    earlier = lax.broadcasted_iota(jnp.int32, (tokens, tokens), 0) < lax.broadcasted_iota(
        jnp.int32, (tokens, tokens), 1
    )
    before = dot(owner_hot.astype(f32).astype(bf16), earlier.astype(f32).astype(bf16), 1, 0)
    rank = jnp.sum(jnp.where(owner_hot, before, 0.0), axis=0, keepdims=True).astype(jnp.int32)
    target = owner * SLOTS + rank
    route = (lax.broadcasted_iota(jnp.int32, (slots, tokens), 0) == target).astype(f32).astype(bf16)
    route_ref[...] = route
    kv = key_ref.shape[1]
    sent_ref[:, :kv] = dot(route, key_ref[...], 1, 0).astype(bf16)
    sent_ref[:, kv : 2 * kv] = dot(route, value_ref[...], 1, 0).astype(bf16)
    code = jnp.broadcast_to((within + 1).astype(f32), (128, tokens)).astype(bf16)
    sent_ref[:, 2 * kv :] = dot(route, code, 1, 1).astype(bf16)


def place_kernel(route_ref, inputs_ref, out_ref):
    out_ref[...] = dot(route_ref[...], inputs_ref[...], 1, 0).astype(bf16)


def weights_kernel(shifts, where_ref, weight_key_ref, weight_value_ref, *refs):
    outs, sems = refs[: len(shifts)], refs[-1]
    width, kv = outs[0].shape[0], weight_key_ref.shape[1]
    copies = []
    for i, s in enumerate(shifts):
        rows = pl.ds(pl.multiple_of(lax.rem(where_ref[3] + s, 4) * width, width), width)
        for j, ref in enumerate((weight_key_ref, weight_value_ref)):
            copies.append(
                pltpu.make_async_copy(
                    ref.at[rows, :], outs[i].at[:, j * kv : (j + 1) * kv], sems.at[2 * i + j]
                )
            )
    for copy in copies:
        copy.start()
    for copy in copies:
        copy.wait()


def pass_kernel(in_ref, out_ref):
    pass


def join_kernel(key_ref, value_ref, out_ref, sems):
    kv = key_ref.shape[1]
    first = pltpu.make_async_copy(key_ref, out_ref.at[:, :kv], sems.at[0])
    second = pltpu.make_async_copy(value_ref, out_ref.at[:, kv:], sems.at[1])
    first.start()
    second.start()
    first.wait()
    second.wait()


def code_row(meta):
    pick = (lax.broadcasted_iota(jnp.int32, (8, 128), 1) == 0).astype(f32).astype(bf16)
    return dot(pick, meta, 1, 1)[:1].astype(jnp.int32)


def select(expanded, code, count, rank):
    total = jnp.where(code == 1, expanded[:rank], 0.0)
    for l in range(1, count):
        total = total + jnp.where(code == l + 1, expanded[l * rank : (l + 1) * rank], 0.0)
    return total


def spread(values, code, count):
    wide = values.astype(f32)
    return jnp.concatenate(
        [jnp.where(code == l + 1, wide, 0.0).astype(bf16) for l in range(count)], axis=0
    )


def back_kernel(got_ref, up_key_ref, up_value_ref, part_ref, code_ref):
    kv = up_key_ref.shape[1]
    code = code_row(got_ref[:, 2 * kv :])
    code_ref[...] = jnp.broadcast_to(code, code_ref.shape)
    part_ref[:16] = select(dot(up_key_ref[...], got_ref[:, :kv], 1, 1), code, 16, 16)
    part_ref[16:] = select(dot(up_value_ref[...], got_ref[:, kv : 2 * kv], 1, 1), code, 16, 16)


def lora_kernel(code_ref, a_ref, b_ref, c_ref, d_ref, down_key_ref, down_value_ref, rows_ref, back_ref):
    code = code_ref[:1]
    total = (a_ref[...] + c_ref[...]) + (b_ref[...] + d_ref[...])
    back = (adapter_scale * total).astype(bf16)
    back_ref[...] = back
    rows = dot(spread(back[:16], code, 16), down_key_ref[...], 0, 0)
    rows = rows + dot(spread(back[16:], code, 16), down_value_ref[...], 0, 0)
    rows_ref[...] = rows.astype(bf16)


def low_kernel(code_ref, rows_ref, down_key_ref, down_value_ref, part_ref):
    code = code_ref[:1]
    part_ref[:16] = select(dot(down_key_ref[...], rows_ref[...], 1, 1), code, 16, 16)
    part_ref[16:] = select(dot(down_value_ref[...], rows_ref[...], 1, 1), code, 16, 16)


def grads_kernel(code_ref, back_ref, a_ref, b_ref, c_ref, d_ref, rows_ref, got_ref,
                 down_key_out, down_value_out, up_key_out, up_value_out):
    code = code_ref[:1]
    kv = up_key_out.shape[1]
    low = ((a_ref[...] + c_ref[...]) + (b_ref[...] + d_ref[...])).astype(bf16)
    down_key_out[...] = dot(spread(back_ref[:16], code, 16), rows_ref[...], 1, 0)
    down_value_out[...] = dot(spread(back_ref[16:], code, 16), rows_ref[...], 1, 0)
    up_key_out[...] = adapter_scale * dot(spread(low[:16], code, 16), got_ref[:, :kv], 1, 0)
    up_value_out[...] = adapter_scale * dot(
        spread(low[16:], code, 16), got_ref[:, kv : 2 * kv], 1, 0
    )


def frozen_kernel(g0, g1, g2, g3, w0, w1, w2, w3, out_ref):
    total = dot(g0[...], w0[...], 1, 1)
    total = total + dot(g1[...], w1[...], 1, 1)
    total = total + dot(g2[...], w2[...], 1, 1)
    out_ref[...] = total + dot(g3[...], w3[...], 1, 1)


def final_kernel(route_ref, rows_ref, frozen_ref, out_ref):
    out_ref[...] = (frozen_ref[...] + dot(route_ref[...], rows_ref[...], 0, 0)).astype(bf16)


def shift_tensor(x, s):
    return lax.ppermute(x, "tensor", [(i, (i + s) % 4) for i in range(4)])


def local(inputs, grad_key, grad_value, weight_key, weight_value, down_key, down_value,
          up_key, up_value, adapter_ids):
    tokens, width = inputs.shape
    kv = grad_key.shape[1]
    owners, rank = 64, down_key.shape[1]
    lr = down_key.shape[0] * rank
    slots = owners * SLOTS
    me = lax.axis_index("adapter")
    t = lax.axis_index("tensor")
    where = jnp.stack([me // 8, me // 2 % 4, me % 2, t]).astype(jnp.int32)
    down_key, down_value = down_key.reshape(lr, width), down_value.reshape(lr, width)
    up_key, up_value = up_key.reshape(lr, kv), up_value.reshape(lr, kv)

    route, sent = call(
        route_kernel, [((slots, tokens), bf16), ((slots, 2 * kv + 128), bf16)], "route"
    )(adapter_ids.reshape(1, tokens), grad_key, grad_value)
    got = lax.all_to_all(sent, "adapter", split_axis=0, concat_axis=0, tiled=True)

    (placed,) = call(place_kernel, [((slots, width), bf16)], "place")(route, inputs)
    held = lax.all_to_all(placed, "adapter", split_axis=0, concat_axis=0, tiled=True)

    def weights(shifts, after=()):
        sliced = call(
            functools.partial(weights_kernel, shifts),
            [((width, 2 * kv), bf16)] * len(shifts), "weights", smem=1, anywhere=True,
            scratch=[pltpu.SemaphoreType.DMA((2 * len(shifts),))], after=after,
        )(where, weight_key, weight_value)
        return {s: shift_tensor(x, s) if s else x for s, x in zip(shifts, sliced)}

    blocks = weights((1, 3))
    part, code = call(
        back_kernel, [((2 * rank, slots), f32), ((8, slots), jnp.int32)], "back",
        after=[blocks[1], blocks[3]],
    )(got, up_key, up_value)
    sums = [part] + [shift_tensor(part, s) for s in (1, 2, 3)]
    rows, back = call(
        lora_kernel, [((slots, width), bf16), ((2 * rank, slots), bf16)], "lora",
    )(code, *sums, down_key, down_value)
    (rows,) = call(pass_kernel, [((slots, width), bf16)], "pass", anywhere=True, alias={0: 0},
                   after=[held])(rows)
    returned = lax.all_to_all(rows, "adapter", split_axis=0, concat_axis=0, tiled=True)

    blocks |= weights((0, 2), after=[back])
    (both,) = call(
        join_kernel, [((tokens, 2 * kv), bf16)], "join", anywhere=True,
        scratch=[pltpu.SemaphoreType.DMA((2,))], after=[back],
    )(grad_key, grad_value)
    every = [both] + [shift_tensor(both, s) for s in (1, 2, 3)]
    (frozen,) = call(frozen_kernel, [((tokens, width), f32)], "frozen")(
        *every, *[blocks[s] for s in range(4)]
    )

    (part,) = call(low_kernel, [((2 * rank, slots), f32)], "low")(code, held, down_key, down_value)
    sums = [part] + [shift_tensor(part, s) for s in (1, 2, 3)]
    grads = call(
        grads_kernel, [((lr, width), f32)] * 2 + [((lr, kv), f32)] * 2, "grads"
    )(code, back, *sums, held, got)
    (input_gradient,) = call(final_kernel, [((tokens, width), bf16)], "final")(
        route, returned, frozen
    )
    count = lr // rank
    return (
        input_gradient,
        grads[0].reshape(count, rank, width),
        grads[1].reshape(count, rank, width),
        grads[2].reshape(count, rank, kv),
        grads[3].reshape(count, rank, kv),
    )


def solution(mesh):
    wide = P("adapter", "tensor")
    frozen = P(None, "tensor")
    adapter = P("adapter", None, "tensor")
    return jax.shard_map(
        local,
        mesh=mesh,
        in_specs=(wide, wide, wide, frozen, frozen, adapter, adapter, adapter, adapter, P("adapter")),
        out_specs=(wide, adapter, adapter, adapter, adapter),
        check_vma=False,
    )
```

```python
import functools

import jax
import jax.numpy as jnp
from jax import lax
from jax.experimental import pallas as pl
from jax.experimental.pallas import tpu as pltpu
from jax.sharding import PartitionSpec as P

adapter_scale = 2.0

SLOTS = 16
MIB = 1 << 20
bf16 = jnp.bfloat16
f32 = jnp.float32


def move(pairs, sem):
    copies = [pltpu.make_async_copy(a, b, sem.at[i]) for i, (a, b) in enumerate(pairs)]
    for copy in copies:
        copy.start()
    for copy in copies:
        copy.wait()


def call(kernel, outs, name, vmem=56, smem=0, scratch=(), after=(), staged=True, loose=()):
    def run(*args):
        count, first = len(args), len(args) + len(after)
        specs = [
            pl.BlockSpec(
                memory_space=pltpu.SMEM if i < smem else pl.ANY if i in loose else pltpu.HBM
            )
            for i in range(count)
        ]
        specs += [pl.BlockSpec(memory_space=pl.ANY)] * len(after)
        held = [pltpu.VMEM(arg.shape, arg.dtype) for arg in args[smem:]] if staged else []
        made = [pltpu.VMEM(s, d) for s, d in outs]
        sems = [pltpu.SemaphoreType.DMA((max(len(held), len(made)),))]

        def body(*refs):
            ins, rest, sem = refs[:count], refs[first:-1], refs[-1]
            results, rest = rest[: len(outs)], rest[len(outs) :]
            results_held, rest = rest[: len(outs)], rest[len(outs) :]
            if staged:
                places, rest = rest[: len(held)], rest[len(held) :]
                move(list(zip(ins[smem:], places)), sem)
                ins = ins[:smem] + places
            kernel(*ins, *results_held, *rest)
            move(list(zip(results_held, results)), sem)

        return pl.pallas_call(
            body,
            out_shape=[jax.ShapeDtypeStruct(s, d) for s, d in outs],
            in_specs=specs,
            out_specs=[pl.BlockSpec(memory_space=pltpu.HBM) for _ in outs],
            scratch_shapes=made + held + list(scratch) + sems,
            compiler_params=pltpu.CompilerParams(vmem_limit_bytes=vmem * MIB),
            name=name,
        )(*args, *after)

    return run


def dot(a, b, ca, cb):
    return lax.dot_general(a, b, (((ca,), (cb,)), ((), ())), preferred_element_type=f32)


def route_kernel(ids_ref, key_ref, value_ref, target_ref, sent_ref):
    ids = ids_ref[...]
    tokens = ids.shape[1]
    slots = sent_ref.shape[0]
    owner = ids >> 4
    within = ids & 15
    owner_hot = lax.broadcasted_iota(jnp.int32, (slots // SLOTS, tokens), 0) == owner
    earlier = lax.broadcasted_iota(jnp.int32, (tokens, tokens), 0) < lax.broadcasted_iota(
        jnp.int32, (tokens, tokens), 1
    )
    before = dot(owner_hot.astype(f32).astype(bf16), earlier.astype(f32).astype(bf16), 1, 0)
    rank = jnp.sum(jnp.where(owner_hot, before, 0.0), axis=0, keepdims=True).astype(jnp.int32)
    target = owner * SLOTS + rank
    target_ref[...] = jnp.broadcast_to(target, target_ref.shape)
    route = routing(target, slots)
    kv = key_ref.shape[1]
    sent_ref[:, :kv] = dot(route, key_ref[...], 1, 0).astype(bf16)
    sent_ref[:, kv : 2 * kv] = dot(route, value_ref[...], 1, 0).astype(bf16)
    code = jnp.broadcast_to((within + 1).astype(f32), (128, tokens)).astype(bf16)
    sent_ref[:, 2 * kv :] = dot(route, code, 1, 1).astype(bf16)


def routing(target, slots):
    place = lax.broadcasted_iota(jnp.int32, (slots, target.shape[1]), 0)
    return (place == target).astype(f32).astype(bf16)


def place_kernel(target_ref, inputs_ref, out_ref, back_ref):
    route = routing(target_ref[:1], out_ref.shape[0])
    out_ref[...] = dot(route, inputs_ref[...], 1, 0).astype(bf16)
    back_ref[...] = route.T


def weights_kernel(shifts, where_ref, weight_key_ref, weight_value_ref, *refs):
    outs, sem = refs[: len(shifts)], refs[-1]
    width, kv = outs[0].shape[0], weight_key_ref.shape[1]
    pairs = []
    for s, out in zip(shifts, outs):
        rows = pl.ds(pl.multiple_of(((where_ref[0] + s) & 3) * width, width), width)
        pairs.append((weight_key_ref.at[rows, :], out.at[:, :kv]))
        pairs.append((weight_value_ref.at[rows, :], out.at[:, kv:]))
    move(pairs, sem)


def join_kernel(key_ref, value_ref, out_ref):
    kv = key_ref.shape[1]
    out_ref[:, :kv] = key_ref[...]
    out_ref[:, kv:] = value_ref[...]


def code_row(meta):
    pick = (lax.broadcasted_iota(jnp.int32, (8, 128), 1) == 0).astype(f32).astype(bf16)
    return dot(pick, meta, 1, 1)[:1].astype(jnp.int32)


def select(expanded, code, count, rank):
    total = jnp.where(code == 1, expanded[:rank], 0.0)
    for l in range(1, count):
        total = total + jnp.where(code == l + 1, expanded[l * rank : (l + 1) * rank], 0.0)
    return total


def spread(values, code, count):
    wide = values.astype(f32)
    return jnp.concatenate(
        [jnp.where(code == l + 1, wide, 0.0).astype(bf16) for l in range(count)], axis=0
    )


def back_kernel(got_ref, up_key_ref, up_value_ref, part_ref, code_ref, kept_ref):
    kv = up_key_ref.shape[1]
    kept_ref[...] = got_ref[:, : 2 * kv]
    code = code_row(got_ref[:, 2 * kv :])
    code_ref[...] = jnp.broadcast_to(code, code_ref.shape)
    part_ref[:16] = select(dot(up_key_ref[...], got_ref[:, :kv], 1, 1), code, 16, 16)
    part_ref[16:] = select(dot(up_value_ref[...], got_ref[:, kv : 2 * kv], 1, 1), code, 16, 16)


def lora_kernel(code_ref, a_ref, b_ref, c_ref, d_ref, down_key_ref, down_value_ref, rows_ref, back_ref):
    code = code_ref[:1]
    total = (a_ref[...] + c_ref[...]) + (b_ref[...] + d_ref[...])
    back = (adapter_scale * total).astype(bf16)
    back_ref[...] = back
    rows = dot(spread(back[:16], code, 16), down_key_ref[...], 0, 0)
    rows = rows + dot(spread(back[16:], code, 16), down_value_ref[...], 0, 0)
    rows_ref[...] = rows.astype(bf16)


def low_kernel(code_ref, rows_ref, down_key_ref, down_value_ref, part_ref, kept_ref):
    kept_ref[...] = rows_ref[...]
    code = code_ref[:1]
    part_ref[:16] = select(dot(down_key_ref[...], rows_ref[...], 1, 1), code, 16, 16)
    part_ref[16:] = select(dot(down_value_ref[...], rows_ref[...], 1, 1), code, 16, 16)


def grads_kernel(code_ref, back_ref, a_ref, b_ref, c_ref, d_ref, rows_ref, got_ref,
                 down_key_out, down_value_out, up_key_out, up_value_out):
    code = code_ref[:1]
    kv = up_key_out.shape[1]
    low = ((a_ref[...] + c_ref[...]) + (b_ref[...] + d_ref[...])).astype(bf16)
    down_key_out[...] = dot(spread(back_ref[:16], code, 16), rows_ref[...], 1, 0)
    down_value_out[...] = dot(spread(back_ref[16:], code, 16), rows_ref[...], 1, 0)
    up_key_out[...] = adapter_scale * dot(spread(low[:16], code, 16), got_ref[:, :kv], 1, 0)
    up_value_out[...] = adapter_scale * dot(
        spread(low[16:], code, 16), got_ref[:, kv : 2 * kv], 1, 0
    )


def frozen_kernel(g0, g1, g2, g3, w0, w1, w2, w3, out_ref):
    total = dot(g0[...], w0[...], 1, 1)
    total = total + dot(g1[...], w1[...], 1, 1)
    total = total + dot(g2[...], w2[...], 1, 1)
    out_ref[...] = total + dot(g3[...], w3[...], 1, 1)


def final_kernel(route_ref, frozen_ref, rows_ref, out_ref, rows, frozen, total, result, sem):
    count, step = rows.shape[0], rows.shape[1]
    arrive = [
        pltpu.make_async_copy(rows_ref.at[pl.ds(i * step, step), :], rows.at[i], sem.at[i])
        for i in range(count)
    ]
    arrive.append(pltpu.make_async_copy(frozen_ref, frozen, sem.at[count]))
    for copy in arrive:
        copy.start()
    for i in range(count):
        arrive[i].wait()
        more = dot(route_ref[:, i * step : (i + 1) * step], rows[i], 1, 0)
        total[...] = more if i == 0 else total[...] + more
    arrive[count].wait()
    half = result.shape[1]
    leave = []
    for i in range(result.shape[0]):
        part = pl.ds(i * half, half)
        result[i] = (total[part, :] + frozen[part, :]).astype(bf16)
        leave.append(pltpu.make_async_copy(result.at[i], out_ref.at[part, :], sem.at[i]))
        leave[i].start()
    for copy in leave:
        copy.wait()


def final(route, frozen, rows, chunks):
    tokens, width = frozen.shape
    slots = rows.shape[0]
    return pl.pallas_call(
        final_kernel,
        out_shape=jax.ShapeDtypeStruct((tokens, width), bf16),
        in_specs=[
            pl.BlockSpec(memory_space=pltpu.VMEM),
            pl.BlockSpec(memory_space=pl.ANY),
            pl.BlockSpec(memory_space=pl.ANY),
        ],
        out_specs=pl.BlockSpec(memory_space=pltpu.HBM),
        scratch_shapes=[
            pltpu.VMEM((chunks, slots // chunks, width), bf16),
            pltpu.VMEM((tokens, width), f32),
            pltpu.VMEM((tokens, width), f32),
            pltpu.VMEM((2, tokens // 2, width), bf16),
            pltpu.SemaphoreType.DMA((chunks + 1,)),
        ],
        compiler_params=pltpu.CompilerParams(vmem_limit_bytes=48 * MIB),
        name="final",
    )(route, frozen, rows)


def hold_kernel(*refs):
    pass


def hold(x, after):
    return pl.pallas_call(
        hold_kernel,
        out_shape=jax.ShapeDtypeStruct(x.shape, x.dtype),
        in_specs=[pl.BlockSpec(memory_space=pltpu.HBM)]
        + [pl.BlockSpec(memory_space=pl.ANY)] * len(after),
        out_specs=pl.BlockSpec(memory_space=pltpu.HBM),
        input_output_aliases={0: 0},
        name="hold",
    )(x, *after)


def shift_tensor(x, s):
    return lax.ppermute(x, "tensor", [(i, (i + s) % 4) for i in range(4)])


def local(inputs, grad_key, grad_value, weight_key, weight_value, down_key, down_value,
          up_key, up_value, adapter_ids):
    tokens, width = inputs.shape
    kv = grad_key.shape[1]
    owners, rank = 64, down_key.shape[1]
    lr = down_key.shape[0] * rank
    slots = owners * SLOTS
    where = lax.axis_index("tensor").astype(jnp.int32).reshape(1)
    down_key, down_value = down_key.reshape(lr, width), down_value.reshape(lr, width)
    up_key, up_value = up_key.reshape(lr, kv), up_value.reshape(lr, kv)

    def weights(shifts, after):
        sliced = call(
            functools.partial(weights_kernel, shifts),
            [((width, 2 * kv), bf16)] * len(shifts), "weights", smem=1, staged=False,
            scratch=[pltpu.SemaphoreType.DMA((2 * len(shifts),))], after=after,
        )(where, weight_key, weight_value)
        return {s: shift_tensor(x, s) if s else x for s, x in zip(shifts, sliced)}

    target, sent = call(
        route_kernel, [((8, tokens), jnp.int32), ((slots, 2 * kv + 128), bf16)], "route"
    )(adapter_ids.reshape(1, tokens), grad_key, grad_value)
    got = lax.all_to_all(sent, "adapter", split_axis=0, concat_axis=0, tiled=True)
    placed, route = call(
        place_kernel, [((slots, width), bf16), ((tokens, slots), bf16)], "place"
    )(target, inputs)
    (both,) = call(join_kernel, [((tokens, 2 * kv), bf16)], "join", after=[target])(
        grad_key, grad_value
    )
    every = [both] + [shift_tensor(both, s) for s in (1, 2, 3)]
    placed = hold(placed, every[1:])
    held = lax.all_to_all(placed, "adapter", split_axis=0, concat_axis=0, tiled=True)
    part, code, got = call(
        back_kernel,
        [((2 * rank, slots), f32), ((8, slots), jnp.int32), ((slots, 2 * kv), bf16)], "back",
        loose=(0,),
    )(got, up_key, up_value)
    blocks = weights((1, 3), [part])
    sums = [part] + [shift_tensor(part, s) for s in (1, 2, 3)]
    rows, back = call(
        lora_kernel, [((slots, width), bf16), ((2 * rank, slots), bf16)], "lora"
    )(code, *sums, down_key, down_value)
    rows = hold(rows, [held, blocks[1], blocks[3]])
    returned = lax.all_to_all(rows, "adapter", split_axis=0, concat_axis=0, tiled=True)
    blocks |= weights((0, 2), [back])
    part, held = call(
        low_kernel, [((2 * rank, slots), f32), ((slots, width), bf16)], "low", loose=(1,)
    )(code, held, down_key, down_value)
    sums = [part] + [shift_tensor(part, s) for s in (1, 2, 3)]
    grads = call(
        grads_kernel, [((lr, width), f32)] * 2 + [((lr, kv), f32)] * 2, "grads"
    )(code, back, *sums, held, got)
    (frozen,) = call(
        frozen_kernel, [((tokens, width), f32)], "frozen", after=[grads[2]]
    )(*every, *[blocks[s] for s in range(4)])
    input_gradient = final(route, frozen, returned, 4)
    count = lr // rank
    return (
        input_gradient,
        grads[0].reshape(count, rank, width),
        grads[1].reshape(count, rank, width),
        grads[2].reshape(count, rank, kv),
        grads[3].reshape(count, rank, kv),
    )


def solution(mesh):
    wide = P("adapter", "tensor")
    frozen = P(None, "tensor")
    adapter = P("adapter", None, "tensor")
    return jax.shard_map(
        local,
        mesh=mesh,
        in_specs=(wide, wide, wide, frozen, frozen, adapter, adapter, adapter, adapter, P("adapter")),
        out_specs=(wide, adapter, adapter, adapter, adapter),
        check_vma=False,
    )
```

```python
import functools

import jax
import jax.numpy as jnp
from jax import lax
from jax.experimental import pallas as pl
from jax.experimental.pallas import tpu as pltpu
from jax.sharding import PartitionSpec as P

adapter_scale = 2.0

SLOTS = 16
MIB = 1 << 20
bf16 = jnp.bfloat16
f32 = jnp.float32


def move(pairs, sem):
    copies = [pltpu.make_async_copy(a, b, sem.at[i]) for i, (a, b) in enumerate(pairs)]
    for copy in copies:
        copy.start()
    for copy in copies:
        copy.wait()


def call(kernel, outs, name, vmem=63, smem=0, scratch=(), after=(), staged=True):
    def run(*args):
        count, first = len(args), len(args) + len(after)
        specs = [
            pl.BlockSpec(
                memory_space=pltpu.SMEM if i < smem else pltpu.HBM
            )
            for i in range(count)
        ]
        specs += [pl.BlockSpec(memory_space=pl.ANY)] * len(after)
        held = [pltpu.VMEM(arg.shape, arg.dtype) for arg in args[smem:]] if staged else []
        made = [pltpu.VMEM(s, d) for s, d in outs]
        sems = [pltpu.SemaphoreType.DMA((max(len(held), len(made)),))]

        def body(*refs):
            ins, rest, sem = refs[:count], refs[first:-1], refs[-1]
            results, rest = rest[: len(outs)], rest[len(outs) :]
            results_held, rest = rest[: len(outs)], rest[len(outs) :]
            if staged:
                places, rest = rest[: len(held)], rest[len(held) :]
                move(list(zip(ins[smem:], places)), sem)
                ins = ins[:smem] + places
            kernel(*ins, *results_held, *rest)
            move(list(zip(results_held, results)), sem)

        return pl.pallas_call(
            body,
            out_shape=[jax.ShapeDtypeStruct(s, d) for s, d in outs],
            in_specs=specs,
            out_specs=[pl.BlockSpec(memory_space=pltpu.HBM) for _ in outs],
            scratch_shapes=made + held + list(scratch) + sems,
            compiler_params=pltpu.CompilerParams(vmem_limit_bytes=vmem * MIB),
            name=name,
        )(*args, *after)

    return run


def dot(a, b, ca, cb):
    return lax.dot_general(a, b, (((ca,), (cb,)), ((), ())), preferred_element_type=f32)


def route_kernel(ids_ref, key_ref, value_ref, target_ref, sent_ref):
    ids = ids_ref[...]
    tokens = ids.shape[1]
    slots = 2 * sent_ref.shape[0]
    owner = ids >> 4
    within = ids & 15
    owner_hot = lax.broadcasted_iota(jnp.int32, (slots // SLOTS, tokens), 0) == owner
    earlier = lax.broadcasted_iota(jnp.int32, (tokens, tokens), 0) < lax.broadcasted_iota(
        jnp.int32, (tokens, tokens), 1
    )
    before = dot(owner_hot.astype(f32).astype(bf16), earlier.astype(f32).astype(bf16), 1, 0)
    rank = jnp.sum(jnp.where(owner_hot, before, 0.0), axis=0, keepdims=True).astype(jnp.int32)
    target = (rank >> 3) * (slots // 2) + owner * (SLOTS // 2) + (rank & 7)
    target_ref[...] = jnp.broadcast_to(target, target_ref.shape)
    route = routing(target, slots)
    kv = key_ref.shape[1]
    code = jnp.broadcast_to((within + 1).astype(f32), (128, tokens)).astype(bf16)
    key = dot(route, key_ref[...], 1, 0).astype(bf16)
    value = dot(route, value_ref[...], 1, 0).astype(bf16)
    code = dot(route, code, 1, 1)
    half = slots // 2
    for h in range(2):
        rows = slice(h * half, (h + 1) * half)
        sent_ref[:, 2 * h * kv : (2 * h + 1) * kv] = key[rows]
        sent_ref[:, (2 * h + 1) * kv : (2 * h + 2) * kv] = value[rows]
    lane = lax.broadcasted_iota(jnp.int32, (half, 128), 1)
    sent_ref[:, 4 * kv :] = jnp.where(lane == 0, code[:half], code[half:]).astype(bf16)


def beside(rows):
    half = rows.shape[0] // 2
    return jnp.concatenate([rows[:half], rows[half:]], axis=1)


def below(rows):
    half = rows.shape[1] // 2
    return jnp.concatenate([rows[:, :half], rows[:, half:]], axis=0)


def routing(target, slots):
    place = lax.broadcasted_iota(jnp.int32, (slots, target.shape[1]), 0)
    return (place == target).astype(f32).astype(bf16)


def place_kernel(target_ref, inputs_ref, out_ref, back_ref):
    route = routing(target_ref[:1], 2 * out_ref.shape[0])
    out_ref[...] = beside(dot(route, inputs_ref[...], 1, 0).astype(bf16))
    back_ref[...] = route.T


def weights_kernel(shifts, where_ref, weight_key_ref, weight_value_ref, *refs):
    outs, sem = refs[: len(shifts)], refs[-1]
    width, kv = outs[0].shape[0], weight_key_ref.shape[1]
    pairs = []
    for s, out in zip(shifts, outs):
        rows = pl.ds(pl.multiple_of(((where_ref[0] + s) & 3) * width, width), width)
        pairs.append((weight_key_ref.at[rows, :], out.at[:, :kv]))
        pairs.append((weight_value_ref.at[rows, :], out.at[:, kv:]))
    move(pairs, sem)


def join_kernel(key_ref, value_ref, out_ref):
    kv = key_ref.shape[1]
    out_ref[:, :kv] = key_ref[...]
    out_ref[:, kv:] = value_ref[...]


def code_row(meta):
    pick = lax.broadcasted_iota(jnp.int32, (8, 128), 0) == lax.broadcasted_iota(
        jnp.int32, (8, 128), 1
    )
    code = dot(pick.astype(f32).astype(bf16), meta, 1, 1).astype(jnp.int32)
    return jnp.concatenate([code[:1], code[1:2]], axis=1)


def select(expanded, code, count, rank):
    total = jnp.where(code == 1, expanded[:rank], 0.0)
    for l in range(1, count):
        total = total + jnp.where(code == l + 1, expanded[l * rank : (l + 1) * rank], 0.0)
    return total


def spread(values, code, count):
    wide = values.astype(f32)
    return jnp.concatenate(
        [jnp.where(code == l + 1, wide, 0.0).astype(bf16) for l in range(count)], axis=0
    )


def back_kernel(got_ref, up_key_ref, up_value_ref, part_ref, code_ref, kept_ref):
    kv = up_key_ref.shape[1]
    kept_ref[...] = below(got_ref[:, : 4 * kv])
    code = code_row(got_ref[:, 4 * kv :])
    code_ref[...] = jnp.broadcast_to(code, code_ref.shape)
    part_ref[:16] = select(dot(up_key_ref[...], kept_ref[:, :kv], 1, 1), code, 16, 16)
    part_ref[16:] = select(dot(up_value_ref[...], kept_ref[:, kv:], 1, 1), code, 16, 16)


def lora_kernel(code_ref, a_ref, b_ref, c_ref, d_ref, down_key_ref, down_value_ref, rows_ref, back_ref):
    code = code_ref[:1]
    total = (a_ref[...] + c_ref[...]) + (b_ref[...] + d_ref[...])
    back = (adapter_scale * total).astype(bf16)
    back_ref[...] = back
    rows = dot(spread(back[:16], code, 16), down_key_ref[...], 0, 0)
    rows = rows + dot(spread(back[16:], code, 16), down_value_ref[...], 0, 0)
    rows_ref[...] = beside(rows.astype(bf16))


def low_kernel(code_ref, rows_ref, down_key_ref, down_value_ref, part_ref, kept_ref):
    kept_ref[...] = below(rows_ref[...])
    code = code_ref[:1]
    part_ref[:16] = select(dot(down_key_ref[...], kept_ref[...], 1, 1), code, 16, 16)
    part_ref[16:] = select(dot(down_value_ref[...], kept_ref[...], 1, 1), code, 16, 16)


def grads_kernel(code_ref, back_ref, a_ref, b_ref, c_ref, d_ref, rows_ref, got_ref,
                 down_key_out, down_value_out, up_key_out, up_value_out):
    code = code_ref[:1]
    kv = up_key_out.shape[1]
    low = ((a_ref[...] + c_ref[...]) + (b_ref[...] + d_ref[...])).astype(bf16)
    down_key_out[...] = dot(spread(back_ref[:16], code, 16), rows_ref[...], 1, 0)
    down_value_out[...] = dot(spread(back_ref[16:], code, 16), rows_ref[...], 1, 0)
    up_key_out[...] = adapter_scale * dot(spread(low[:16], code, 16), got_ref[:, :kv], 1, 0)
    up_value_out[...] = adapter_scale * dot(
        spread(low[16:], code, 16), got_ref[:, kv : 2 * kv], 1, 0
    )


def frozen_kernel(g0, g1, g2, g3, w0, w1, w2, w3, out_ref):
    total = dot(g0[...], w0[...], 1, 1)
    total = total + dot(g1[...], w1[...], 1, 1)
    total = total + dot(g2[...], w2[...], 1, 1)
    out_ref[...] = total + dot(g3[...], w3[...], 1, 1)


def final_kernel(columns, route_ref, frozen_ref, rows_ref, out_ref, route, frozen, rows, result, sem, sem_out):
    half, width = rows.shape[0], frozen.shape[1]
    arrive = [
        pltpu.make_async_copy(a, b, sem.at[i])
        for i, (a, b) in enumerate([(route_ref, route), (rows_ref, rows), (frozen_ref, frozen)])
    ]
    leave = []
    for copy in arrive:
        copy.start()
    arrive[0].wait()
    arrive[1].wait()
    for i in range(result.shape[0]):
        at = i * columns
        total = dot(route[:, :half], rows[:, at : at + columns], 1, 0)
        total = total + dot(route[:, half:], rows[:, width + at : width + at + columns], 1, 0)
        if i == 0:
            arrive[2].wait()
        result[i] = (total + frozen[:, at : at + columns]).astype(bf16)
        leave.append(
            pltpu.make_async_copy(result.at[i], out_ref.at[:, pl.ds(at, columns)], sem_out.at[i])
        )
        leave[i].start()
    for copy in leave:
        copy.wait()


def final(route, frozen, rows, columns):
    tokens, width = frozen.shape
    count = width // columns
    return pl.pallas_call(
        functools.partial(final_kernel, columns),
        out_shape=jax.ShapeDtypeStruct((tokens, width), bf16),
        in_specs=[pl.BlockSpec(memory_space=pltpu.HBM)] * 3,
        out_specs=pl.BlockSpec(memory_space=pltpu.HBM),
        scratch_shapes=[
            pltpu.VMEM(route.shape, bf16),
            pltpu.VMEM(frozen.shape, f32),
            pltpu.VMEM(rows.shape, bf16),
            pltpu.VMEM((count, tokens, columns), bf16),
            pltpu.SemaphoreType.DMA((3,)),
            pltpu.SemaphoreType.DMA((count,)),
        ],
        compiler_params=pltpu.CompilerParams(vmem_limit_bytes=63 * MIB),
        name="final",
    )(route, frozen, rows)


def hold_kernel(*refs):
    pass


def hold(x, after):
    return pl.pallas_call(
        hold_kernel,
        out_shape=jax.ShapeDtypeStruct(x.shape, x.dtype),
        in_specs=[pl.BlockSpec(memory_space=pltpu.HBM)]
        + [pl.BlockSpec(memory_space=pl.ANY)] * len(after),
        out_specs=pl.BlockSpec(memory_space=pltpu.HBM),
        input_output_aliases={0: 0},
        name="hold",
    )(x, *after)


def shift_tensor(x, s):
    return lax.ppermute(x, "tensor", [(i, (i + s) % 4) for i in range(4)])


def local(inputs, grad_key, grad_value, weight_key, weight_value, down_key, down_value,
          up_key, up_value, adapter_ids):
    tokens, width = inputs.shape
    kv = grad_key.shape[1]
    owners, rank = 64, down_key.shape[1]
    lr = down_key.shape[0] * rank
    slots = owners * SLOTS
    where = lax.axis_index("tensor").astype(jnp.int32).reshape(1)
    down_key, down_value = down_key.reshape(lr, width), down_value.reshape(lr, width)
    up_key, up_value = up_key.reshape(lr, kv), up_value.reshape(lr, kv)

    def weights(shifts, after):
        sliced = call(
            functools.partial(weights_kernel, shifts),
            [((width, 2 * kv), bf16)] * len(shifts), "weights", smem=1, staged=False,
            scratch=[pltpu.SemaphoreType.DMA((2 * len(shifts),))], after=after,
        )(where, weight_key, weight_value)
        return {s: shift_tensor(x, s) if s else x for s, x in zip(shifts, sliced)}

    target, sent = call(
        route_kernel, [((8, tokens), jnp.int32), ((slots // 2, 4 * kv + 128), bf16)], "route"
    )(adapter_ids.reshape(1, tokens), grad_key, grad_value)
    got = lax.all_to_all(sent, "adapter", split_axis=0, concat_axis=0, tiled=True)
    placed, route = call(
        place_kernel, [((slots // 2, 2 * width), bf16), ((tokens, slots), bf16)], "place"
    )(target, inputs)
    (both,) = call(join_kernel, [((tokens, 2 * kv), bf16)], "join", after=[target])(
        grad_key, grad_value
    )
    every = [both] + [shift_tensor(both, s) for s in (1, 2, 3)]
    placed = hold(placed, [every[1], every[3]])
    held = lax.all_to_all(placed, "adapter", split_axis=0, concat_axis=0, tiled=True)
    part, code, got = call(
        back_kernel,
        [((2 * rank, slots), f32), ((8, slots), jnp.int32), ((slots, 2 * kv), bf16)], "back",
    )(got, up_key, up_value)
    blocks = weights((1, 3), [part])
    sums = [part] + [shift_tensor(part, s) for s in (1, 2, 3)]
    rows, back = call(
        lora_kernel, [((slots // 2, 2 * width), bf16), ((2 * rank, slots), bf16)], "lora"
    )(code, *sums, down_key, down_value)
    rows = hold(rows, [held, blocks[1], blocks[3], every[2]])
    returned = lax.all_to_all(rows, "adapter", split_axis=0, concat_axis=0, tiled=True)
    blocks |= weights((0, 2), [back])
    part, held = call(
        low_kernel, [((2 * rank, slots), f32), ((slots, width), bf16)], "low"
    )(code, held, down_key, down_value)
    sums = [part] + [shift_tensor(part, s) for s in (1, 2, 3)]
    grads = call(
        grads_kernel, [((lr, width), f32)] * 2 + [((lr, kv), f32)] * 2, "grads"
    )(code, back, *sums, held, got)
    (frozen,) = call(
        frozen_kernel, [((tokens, width), f32)], "frozen", after=[grads[2]]
    )(*every, *[blocks[s] for s in range(4)])
    input_gradient = final(route, frozen, returned, 256)
    count = lr // rank
    return (
        input_gradient,
        grads[0].reshape(count, rank, width),
        grads[1].reshape(count, rank, width),
        grads[2].reshape(count, rank, kv),
        grads[3].reshape(count, rank, kv),
    )


def solution(mesh):
    wide = P("adapter", "tensor")
    frozen = P(None, "tensor")
    adapter = P("adapter", None, "tensor")
    return jax.shard_map(
        local,
        mesh=mesh,
        in_specs=(wide, wide, wide, frozen, frozen, adapter, adapter, adapter, adapter, P("adapter")),
        out_specs=(wide, adapter, adapter, adapter, adapter),
        check_vma=False,
    )
```

```python
import functools

import jax
import jax.numpy as jnp
from jax import lax
from jax.experimental import pallas as pl
from jax.experimental.pallas import tpu as pltpu
from jax.sharding import PartitionSpec as P

adapter_scale = 2.0

SLOTS = 16
MIB = 1 << 20
bf16 = jnp.bfloat16
f32 = jnp.float32


def move(pairs, sem):
    copies = [pltpu.make_async_copy(a, b, sem.at[i]) for i, (a, b) in enumerate(pairs)]
    for copy in copies:
        copy.start()
    for copy in copies:
        copy.wait()


def call(kernel, outs, name, vmem=63, smem=0, scratch=(), after=(), staged=True):
    def run(*args):
        count, first = len(args), len(args) + len(after)
        specs = [
            pl.BlockSpec(
                memory_space=pltpu.SMEM if i < smem else pltpu.HBM
            )
            for i in range(count)
        ]
        specs += [pl.BlockSpec(memory_space=pl.ANY)] * len(after)
        held = [pltpu.VMEM(arg.shape, arg.dtype) for arg in args[smem:]] if staged else []
        made = [pltpu.VMEM(s, d) for s, d in outs]
        sems = [pltpu.SemaphoreType.DMA((max(len(held), len(made)),))]

        def body(*refs):
            ins, rest, sem = refs[:count], refs[first:-1], refs[-1]
            results, rest = rest[: len(outs)], rest[len(outs) :]
            results_held, rest = rest[: len(outs)], rest[len(outs) :]
            if staged:
                places, rest = rest[: len(held)], rest[len(held) :]
                move(list(zip(ins[smem:], places)), sem)
                ins = ins[:smem] + places
            kernel(*ins, *results_held, *rest)
            move(list(zip(results_held, results)), sem)

        return pl.pallas_call(
            body,
            out_shape=[jax.ShapeDtypeStruct(s, d) for s, d in outs],
            in_specs=specs,
            out_specs=[pl.BlockSpec(memory_space=pltpu.HBM) for _ in outs],
            scratch_shapes=made + held + list(scratch) + sems,
            compiler_params=pltpu.CompilerParams(vmem_limit_bytes=vmem * MIB),
            name=name,
        )(*args, *after)

    return run


def dot(a, b, ca, cb):
    return lax.dot_general(a, b, (((ca,), (cb,)), ((), ())), preferred_element_type=f32)


def route_kernel(ids_ref, key_ref, value_ref, target_ref, sent_ref):
    ids = ids_ref[...]
    tokens = ids.shape[1]
    slots = 2 * sent_ref.shape[0]
    owner = ids >> 4
    within = ids & 15
    owner_hot = lax.broadcasted_iota(jnp.int32, (slots // SLOTS, tokens), 0) == owner
    earlier = lax.broadcasted_iota(jnp.int32, (tokens, tokens), 0) < lax.broadcasted_iota(
        jnp.int32, (tokens, tokens), 1
    )
    before = dot(owner_hot.astype(f32).astype(bf16), earlier.astype(f32).astype(bf16), 1, 0)
    rank = jnp.sum(jnp.where(owner_hot, before, 0.0), axis=0, keepdims=True).astype(jnp.int32)
    target = (rank >> 3) * (slots // 2) + owner * (SLOTS // 2) + (rank & 7)
    target_ref[...] = jnp.broadcast_to(target, target_ref.shape)
    route = routing(target, slots)
    kv = key_ref.shape[1]
    code = jnp.broadcast_to((within + 1).astype(f32), (128, tokens)).astype(bf16)
    key = dot(route, key_ref[...], 1, 0).astype(bf16)
    value = dot(route, value_ref[...], 1, 0).astype(bf16)
    code = dot(route, code, 1, 1)
    half = slots // 2
    for h in range(2):
        rows = slice(h * half, (h + 1) * half)
        sent_ref[:, 2 * h * kv : (2 * h + 1) * kv] = key[rows]
        sent_ref[:, (2 * h + 1) * kv : (2 * h + 2) * kv] = value[rows]
    lane = lax.broadcasted_iota(jnp.int32, (half, 128), 1)
    sent_ref[:, 4 * kv :] = jnp.where(lane == 0, code[:half], code[half:]).astype(bf16)


def beside(rows):
    half = rows.shape[0] // 2
    return jnp.concatenate([rows[:half], rows[half:]], axis=1)


def below(rows):
    half = rows.shape[1] // 2
    return jnp.concatenate([rows[:, :half], rows[:, half:]], axis=0)


def routing(target, slots):
    place = lax.broadcasted_iota(jnp.int32, (slots, target.shape[1]), 0)
    return (place == target).astype(f32).astype(bf16)


def place_kernel(target_ref, inputs_ref, out_ref, back_ref):
    route = routing(target_ref[:1], 2 * out_ref.shape[0])
    out_ref[...] = beside(dot(route, inputs_ref[...], 1, 0).astype(bf16))
    back_ref[...] = route.T


def weights_kernel(shifts, where_ref, weight_key_ref, weight_value_ref, *refs):
    outs, sem = refs[: len(shifts)], refs[-1]
    width, kv = outs[0].shape[0], weight_key_ref.shape[1]
    pairs = []
    for s, out in zip(shifts, outs):
        rows = pl.ds(pl.multiple_of(((where_ref[0] + s) & 3) * width, width), width)
        pairs.append((weight_key_ref.at[rows, :], out.at[:, :kv]))
        pairs.append((weight_value_ref.at[rows, :], out.at[:, kv:]))
    move(pairs, sem)


def join_kernel(key_ref, value_ref, out_ref):
    kv = key_ref.shape[1]
    out_ref[:, :kv] = key_ref[...]
    out_ref[:, kv:] = value_ref[...]


def code_row(meta):
    pick = lax.broadcasted_iota(jnp.int32, (8, 128), 0) == lax.broadcasted_iota(
        jnp.int32, (8, 128), 1
    )
    code = dot(pick.astype(f32).astype(bf16), meta, 1, 1).astype(jnp.int32)
    return jnp.concatenate([code[:1], code[1:2]], axis=1)


def select(expanded, code, count, rank):
    total = jnp.where(code == 1, expanded[:rank], 0.0)
    for l in range(1, count):
        total = total + jnp.where(code == l + 1, expanded[l * rank : (l + 1) * rank], 0.0)
    return total


def spread(values, code, count):
    wide = values.astype(f32)
    return jnp.concatenate(
        [jnp.where(code == l + 1, wide, 0.0).astype(bf16) for l in range(count)], axis=0
    )


def back_kernel(got_ref, up_key_ref, up_value_ref, part_ref, code_ref, kept_ref):
    kv = up_key_ref.shape[1]
    kept_ref[...] = below(got_ref[:, : 4 * kv])
    code = code_row(got_ref[:, 4 * kv :])
    code_ref[...] = jnp.broadcast_to(code, code_ref.shape)
    part_ref[:16] = select(dot(up_key_ref[...], kept_ref[:, :kv], 1, 1), code, 16, 16)
    part_ref[16:] = select(dot(up_value_ref[...], kept_ref[:, kv:], 1, 1), code, 16, 16)


def lora_kernel(code_ref, a_ref, b_ref, c_ref, d_ref, down_key_ref, down_value_ref, rows_ref, back_ref):
    code = code_ref[:1]
    total = (a_ref[...] + c_ref[...]) + (b_ref[...] + d_ref[...])
    back = (adapter_scale * total).astype(bf16)
    back_ref[...] = back
    rows = dot(spread(back[:16], code, 16), down_key_ref[...], 0, 0)
    rows = rows + dot(spread(back[16:], code, 16), down_value_ref[...], 0, 0)
    rows_ref[...] = beside(rows.astype(bf16))


def low_kernel(code_ref, rows_ref, down_key_ref, down_value_ref, part_ref, kept_ref):
    kept_ref[...] = below(rows_ref[...])
    code = code_ref[:1]
    part_ref[:16] = select(dot(down_key_ref[...], kept_ref[...], 1, 1), code, 16, 16)
    part_ref[16:] = select(dot(down_value_ref[...], kept_ref[...], 1, 1), code, 16, 16)


def grads_kernel(code_ref, back_ref, a_ref, b_ref, c_ref, d_ref, rows_ref, got_ref,
                 down_key_out, down_value_out, up_key_out, up_value_out):
    code = code_ref[:1]
    kv = up_key_out.shape[1]
    low = ((a_ref[...] + c_ref[...]) + (b_ref[...] + d_ref[...])).astype(bf16)
    down_key_out[...] = dot(spread(back_ref[:16], code, 16), rows_ref[...], 1, 0)
    down_value_out[...] = dot(spread(back_ref[16:], code, 16), rows_ref[...], 1, 0)
    up_key_out[...] = adapter_scale * dot(spread(low[:16], code, 16), got_ref[:, :kv], 1, 0)
    up_value_out[...] = adapter_scale * dot(
        spread(low[16:], code, 16), got_ref[:, kv : 2 * kv], 1, 0
    )


def frozen_kernel(g0, g1, g2, g3, w0, w1, w2, w3, out_ref):
    total = dot(g0[...], w0[...], 1, 1)
    total = total + dot(g1[...], w1[...], 1, 1)
    total = total + dot(g2[...], w2[...], 1, 1)
    out_ref[...] = total + dot(g3[...], w3[...], 1, 1)


def final_kernel(columns, route_ref, frozen_ref, rows_ref, out_ref, route, frozen, rows, result, sem, sem_out):
    half, width = rows.shape[0], frozen.shape[1]
    arrive = [
        pltpu.make_async_copy(a, b, sem.at[i])
        for i, (a, b) in enumerate([(route_ref, route), (rows_ref, rows), (frozen_ref, frozen)])
    ]
    leave = []
    for copy in arrive:
        copy.start()
    arrive[0].wait()
    arrive[1].wait()
    for i in range(result.shape[0]):
        at = i * columns
        total = dot(route[:, :half], rows[:, at : at + columns], 1, 0)
        total = total + dot(route[:, half:], rows[:, width + at : width + at + columns], 1, 0)
        if i == 0:
            arrive[2].wait()
        result[i] = (total + frozen[:, at : at + columns]).astype(bf16)
        leave.append(
            pltpu.make_async_copy(result.at[i], out_ref.at[:, pl.ds(at, columns)], sem_out.at[i])
        )
        leave[i].start()
    for copy in leave:
        copy.wait()


def final(route, frozen, rows, columns):
    tokens, width = frozen.shape
    count = width // columns
    return pl.pallas_call(
        functools.partial(final_kernel, columns),
        out_shape=jax.ShapeDtypeStruct((tokens, width), bf16),
        in_specs=[pl.BlockSpec(memory_space=pltpu.HBM)] * 3,
        out_specs=pl.BlockSpec(memory_space=pltpu.HBM),
        scratch_shapes=[
            pltpu.VMEM(route.shape, bf16),
            pltpu.VMEM(frozen.shape, f32),
            pltpu.VMEM(rows.shape, bf16),
            pltpu.VMEM((count, tokens, columns), bf16),
            pltpu.SemaphoreType.DMA((3,)),
            pltpu.SemaphoreType.DMA((count,)),
        ],
        compiler_params=pltpu.CompilerParams(vmem_limit_bytes=63 * MIB),
        name="final",
    )(route, frozen, rows)


def hold_kernel(*refs):
    pass


def hold(x, after):
    return pl.pallas_call(
        hold_kernel,
        out_shape=jax.ShapeDtypeStruct(x.shape, x.dtype),
        in_specs=[pl.BlockSpec(memory_space=pltpu.HBM)]
        + [pl.BlockSpec(memory_space=pl.ANY)] * len(after),
        out_specs=pl.BlockSpec(memory_space=pltpu.HBM),
        input_output_aliases={0: 0},
        name="hold",
    )(x, *after)


def shift_tensor(x, s):
    return lax.ppermute(x, "tensor", [(i, (i + s) % 4) for i in range(4)])


def local(inputs, grad_key, grad_value, weight_key, weight_value, down_key, down_value,
          up_key, up_value, adapter_ids):
    tokens, width = inputs.shape
    kv = grad_key.shape[1]
    owners, rank = 64, down_key.shape[1]
    lr = down_key.shape[0] * rank
    slots = owners * SLOTS
    where = lax.axis_index("tensor").astype(jnp.int32).reshape(1)
    down_key, down_value = down_key.reshape(lr, width), down_value.reshape(lr, width)
    up_key, up_value = up_key.reshape(lr, kv), up_value.reshape(lr, kv)

    def weights(shifts, after):
        sliced = call(
            functools.partial(weights_kernel, shifts),
            [((width, 2 * kv), bf16)] * len(shifts), "weights", smem=1, staged=False,
            scratch=[pltpu.SemaphoreType.DMA((2 * len(shifts),))], after=after,
        )(where, weight_key, weight_value)
        return {s: shift_tensor(x, s) if s else x for s, x in zip(shifts, sliced)}

    target, sent = call(
        route_kernel, [((8, tokens), jnp.int32), ((slots // 2, 4 * kv + 128), bf16)], "route"
    )(adapter_ids.reshape(1, tokens), grad_key, grad_value)
    got = lax.all_to_all(sent, "adapter", split_axis=0, concat_axis=0, tiled=True)
    placed, route = call(
        place_kernel, [((slots // 2, 2 * width), bf16), ((tokens, slots), bf16)], "place"
    )(target, inputs)
    (both,) = call(join_kernel, [((tokens, 2 * kv), bf16)], "join", after=[target])(
        grad_key, grad_value
    )
    every = [both] + [shift_tensor(both, s) for s in (1, 2, 3)]
    placed = hold(placed, every[1:])
    held = lax.all_to_all(placed, "adapter", split_axis=0, concat_axis=0, tiled=True)
    part, code, got = call(
        back_kernel,
        [((2 * rank, slots), f32), ((8, slots), jnp.int32), ((slots, 2 * kv), bf16)], "back",
    )(got, up_key, up_value)
    blocks = weights((1, 3), [part])
    sums = [part] + [shift_tensor(part, s) for s in (1, 2, 3)]
    rows, back = call(
        lora_kernel, [((slots // 2, 2 * width), bf16), ((2 * rank, slots), bf16)], "lora"
    )(code, *sums, down_key, down_value)
    rows = hold(rows, [held, blocks[1], blocks[3]])
    returned = lax.all_to_all(rows, "adapter", split_axis=0, concat_axis=0, tiled=True)
    blocks |= weights((0, 2), [back])
    part, held = call(
        low_kernel, [((2 * rank, slots), f32), ((slots, width), bf16)], "low"
    )(code, held, down_key, down_value)
    sums = [part] + [shift_tensor(part, s) for s in (1, 2, 3)]
    grads = call(
        grads_kernel, [((lr, width), f32)] * 2 + [((lr, kv), f32)] * 2, "grads"
    )(code, back, *sums, held, got)
    (frozen,) = call(
        frozen_kernel, [((tokens, width), f32)], "frozen", after=[grads[2]]
    )(*every, *[blocks[s] for s in range(4)])
    input_gradient = final(route, frozen, returned, 256)
    count = lr // rank
    return (
        input_gradient,
        grads[0].reshape(count, rank, width),
        grads[1].reshape(count, rank, width),
        grads[2].reshape(count, rank, kv),
        grads[3].reshape(count, rank, kv),
    )


def solution(mesh):
    wide = P("adapter", "tensor")
    frozen = P(None, "tensor")
    adapter = P("adapter", None, "tensor")
    return jax.shard_map(
        local,
        mesh=mesh,
        in_specs=(wide, wide, wide, frozen, frozen, adapter, adapter, adapter, adapter, P("adapter")),
        out_specs=(wide, adapter, adapter, adapter, adapter),
        check_vma=False,
    )
```
